32 devices in a mesh: dp: 8 (over z, x), expert: 2 (over core), ffn: 2 (over y).
Axes of the slice: x: 2, y: 2, z: 4, core: 2. Of those that a mesh axis runs over, the one named last changes fastest.
Arguments:
- grad_rows: bfloat16 [1024, 6144], P('dp', 'ffn'), may hold values from -80 to 80
- gate_probs: float32 [1024, 2], P('dp'), may hold values from 0.1 to 1
- expert_ids: int32 [1024, 2], P('dp'), may hold values from 0 to 3, all different within a row; in each aligned block of 128 rows (0 to 127, 128 to 255, ...) at most 72 rows name the same one
- gate_pre: bfloat16 [4, 576, 8192], P('expert', 'ffn', 'dp'), may hold values from -6 to 6
- up_pre: bfloat16 [4, 576, 8192], P('expert', 'ffn', 'dp'), may hold values from -40 to 40
- down_weight: bfloat16 [4, 8192, 6144], P('expert', 'dp', 'ffn'), may hold values from -0.0625 to 0.0625
Outputs:
- down_grad: bfloat16 [4, 8192, 6144], P('expert', 'dp', 'ffn')
- gate_grad: bfloat16 [4, 576, 8192], P('expert', 'ffn', 'dp')
- up_grad: bfloat16 [4, 576, 8192], P('expert', 'ffn', 'dp')
The draws below stay inside these ranges and needn't reach their ends.
Inputs may be any that keep to these rules, and one draw needn't show every extreme that they name: `expert_ids`: in the 128 tokens of one index of dp no expert is named by more than 72 routes, a bound that some block reaches; a token's two routes name different experts.
All inputs are finite; a program needn't handle non-finite values.
Results may differ from the reference program's by a relative error of at most 0.019.
Values may be sent and summed in bfloat16 or wider, within the bound.
A program may use at most 128 MiB of HBM per device.

```python
import math
import jax
import jax.numpy as jnp
import numpy as np
from jax import lax

D = 6144
FF = 8192
TOP = 2
TOK_DEV = 128
EXPERTS = 4
CAP = 72
ROWS = 576
TOKENS = 1024
N_DP = 8
N_FFN = 2


def draw_grad_rows(key, part):
    key_values, key_scale = jax.random.split(key, 2)
    position = jnp.arange(TOKENS, dtype=jnp.float32) / TOKENS
    row_scale = 0.4 * jnp.power(3.0, position) * jnp.power(10.0, jax.random.uniform(key_scale, (TOKENS,), jnp.float32))
    values_drawn = jax.random.normal(key_values, (TOKENS, D), jnp.float32)
    values_drawn = jnp.clip(values_drawn, -6.0, 6.0)
    return (row_scale[:, None] * values_drawn).astype(jnp.bfloat16)


def draw_up_pre(key, part):
    key_values = jax.random.fold_in(jax.random.fold_in(key, 17), 0)
    position = jnp.arange(FF, dtype=jnp.float32) / FF
    column_scale = 0.3 * jnp.power(10.0, position)
    values_drawn = jnp.clip(jax.random.normal(key_values, (EXPERTS, ROWS, FF), jnp.float32), -6.0, 6.0)
    return (column_scale[None, None, :] * values_drawn).astype(jnp.bfloat16)


def block_levels(stream_key, dims, cuts, low, largest):
    gain = 1.0
    for dim, shards_of in cuts:
        steps = jax.random.uniform(jax.random.fold_in(jax.random.fold_in(stream_key, 6), dim), (shards_of,), jnp.float32, low / len(cuts), largest / len(cuts))
        gain = gain * jnp.repeat(jnp.exp(steps), dims[dim] // shards_of).reshape((-1,) + (1,) * (len(dims) - 1 - dim))
    return gain


def routed_block(own_key, own, number, rows, count, top, most, slope):
    sequence = jax.random.permutation(own_key, count)
    crowded, ordinary = portions_of(count, rows * top, most, slope, True), portions_of(count, rows * top, most, slope, False)
    places = jnp.arange(count)

    def named(sizes, rotation):
        used = int((sizes > 0).sum())
        fixed = max(1, used // 4)
        shifted = fixed + (places - fixed + rotation * (used - fixed)) % max(1, count - fixed)
        return jnp.zeros((count,), jnp.int32).at[sequence[jnp.where(places < fixed, places, shifted)]].set(jnp.asarray(sizes, jnp.int32))

    sizes = jnp.where(number % 4 == 0, named(crowded, number // 4), named(ordinary, number - number // 4 - 1))
    mixed = jax.random.permutation(jax.random.fold_in(own, 3), count)
    giver, taker = mixed[0:count // 2 * 2:2], mixed[1:count // 2 * 2:2]
    room = jnp.minimum(sizes[giver] - 1, most - sizes[taker]) // 2
    room = jnp.where((giver == sequence[0]) | (taker == sequence[0]) | (sizes[taker] == 0), 0, jnp.maximum(room, 0))
    shifted = jax.random.randint(jax.random.fold_in(own, 4), (count // 2,), 0, 1 << 20) % (room + 1)
    sizes = sizes.at[giver].add(-shifted).at[taker].add(shifted)
    members = jnp.searchsorted(jnp.cumsum(sizes), jnp.arange(rows * top), side="right").astype(jnp.int32)
    listing = members.reshape(top, rows).T
    listing = listing[jax.random.permutation(jax.random.fold_in(own, 1), rows)]
    rotation = jax.random.randint(jax.random.fold_in(own, 2), (rows, 1), 0, top)
    return jnp.take_along_axis(listing, (jnp.arange(top)[None, :] + rotation) % top, axis=1)


def portions_of(count, total, most, slope, full):
    weights = [(1 << 20) // math.isqrt(grade ** slope) + 1 for grade in range(1, count + 1)]
    largest = most if full else min(most, max(-(-total // count), total * weights[0] // sum(weights)))
    least = 1 if total - largest >= count - 1 else 0
    counts, rest = [largest] + [least] * (count - 1), total - largest - least * (count - 1)
    while rest > 0:
        movable = [i for i in range(1, count) if counts[i] < largest] or [i for i in range(1, count) if counts[i] < most]
        pool, budget = sum([weights[i] for i in movable]), rest
        for i in movable:
            addition = min(most - counts[i], max(1, budget * weights[i] // pool), rest)
            counts[i] = counts[i] + addition
            rest = rest - addition
    return np.array(counts)


def noise(stream_key, dims, deviation, limit, cuts=(), held_as=jnp.bfloat16):
    drawn = jax.random.normal(stream_key, dims, jnp.float32) * deviation
    if len(cuts) > 0:
        drawn = block_levels(stream_key, dims, cuts, -0.22, 0.18) * drawn
    return jnp.clip(drawn, min=-limit, max=limit).astype(held_as)


def setup_inputs(seed: int = 0) -> dict:
    key_of = jax.random.split(jax.random.key(seed), 7)
    grad_rows = draw_grad_rows(jax.random.fold_in(key_of[6], 71), 0)
    gate_probs = jnp.clip(0.1 + 0.9 * jax.random.uniform(key_of[1], (TOKENS, TOP), jnp.float32) ** block_levels(key_of[1], (TOKENS, TOP), ((0, 8),), -0.2, 0.2), 0.1, 1.0)
    expert_ids_keys = jax.random.split(jax.random.fold_in(key_of[2], 1), TOKENS // TOK_DEV)
    expert_ids_turns = jax.random.permutation(jax.random.fold_in(key_of[2], 3), TOKENS // TOK_DEV)
    expert_ids = jax.vmap(lambda own, number: routed_block(jax.random.fold_in(key_of[2], 2), own, number, TOK_DEV, EXPERTS, TOP, CAP, 2))(expert_ids_keys, expert_ids_turns).reshape((TOKENS, TOP))
    gate_pre = noise(key_of[3], (EXPERTS, ROWS, FF), 1.0, 6.0, ((0, 2), (1, 2), (2, 8)))
    up_pre = draw_up_pre(jax.random.fold_in(key_of[6], 71), 0)
    down_weight = noise(key_of[5], (EXPERTS, FF, D), FF ** -0.5, 0.0625, ((0, 2), (1, 8), (2, 2)))
    return {"grad_rows": grad_rows, "gate_probs": gate_probs, "expert_ids": expert_ids, "gate_pre": gate_pre, "up_pre": up_pre, "down_weight": down_weight}


def slot_table(expert_ids):
    route_ids = expert_ids.reshape(N_DP, TOK_DEV * TOP)
    one_hot = (route_ids[:, :, None] == jnp.arange(EXPERTS, dtype=jnp.int32)[None, None, :]).astype(jnp.int32)
    earlier = jnp.cumsum(one_hot, axis=1) - one_hot
    return lax.optimization_barrier(jnp.sum(earlier * one_hot, axis=2)).reshape(TOKENS, TOP).astype(jnp.int32)

def reference(grad_rows, gate_probs, expert_ids, gate_pre, up_pre, down_weight):
    slot_index = slot_table(expert_ids)
    source = (jnp.arange(TOKENS, dtype=jnp.int32) // TOK_DEV).astype(jnp.int32)
    row_index = (source[:, None] * CAP + slot_index).astype(jnp.int32)
    scaled = gate_probs[:, :, None] * grad_rows.astype(jnp.float32)[:, None, :]
    dispatched = jnp.zeros((EXPERTS, ROWS, D), jnp.float32).at[expert_ids, row_index].add(scaled)
    dispatched = dispatched.astype(jnp.bfloat16)
    gate_value = gate_pre.astype(jnp.float32)
    up_value = up_pre.astype(jnp.float32)
    sigmoid_gate = jax.nn.sigmoid(gate_value)
    silu_gate = gate_value * sigmoid_gate
    hidden = (silu_gate * up_value).astype(jnp.bfloat16)
    block_width = D // N_FFN
    hidden_grad = jnp.zeros((EXPERTS, ROWS, FF), jnp.float32)
    for block in range(N_FFN):
        lower = block * block_width
        term = jnp.einsum('erd,efd->erf', dispatched[:, :, lower:lower + block_width].astype(jnp.float32), down_weight[:, :, lower:lower + block_width].astype(jnp.float32))
        rounded = lax.optimization_barrier(term.astype(jnp.bfloat16))
        hidden_grad = hidden_grad + rounded.astype(jnp.float32)
    gate_grad = (hidden_grad * up_value * sigmoid_gate * (1.0 + gate_value * (1.0 - sigmoid_gate))).astype(jnp.bfloat16)
    up_grad = (hidden_grad * silu_gate).astype(jnp.bfloat16)
    weight_grad = jnp.einsum('erf,erd->efd', hidden.astype(jnp.float32), dispatched.astype(jnp.float32))
    squares = jnp.sum(jnp.square(weight_grad))
    clip_limit = jnp.float32(0.5 * (float(EXPERTS) * float(FF) * float(D)) ** 0.5)
    factor = clip_limit / jnp.maximum(jnp.sqrt(squares), clip_limit)
    down_grad = (weight_grad * factor).astype(jnp.bfloat16)
    return (down_grad, gate_grad, up_grad)
```

```python
import functools
import math

import jax
import jax.numpy as jnp
from jax import lax
from jax.experimental import pallas as pl
from jax.experimental.pallas import tpu as pltpu
from jax.sharding import PartitionSpec as P

CAP = 72
MESH = pl.DeviceIdType.MESH
F32 = jnp.float32
BF16 = jnp.bfloat16


def slot_table(route_ids, experts_total):
    tokens_here, routes = route_ids.shape
    flat_ids = route_ids.reshape(tokens_here * routes)
    one_hot = (flat_ids[:, None] == jnp.arange(experts_total, dtype=jnp.int32)[None, :]).astype(
        jnp.int32
    )
    earlier = jnp.cumsum(one_hot, axis=0) - one_hot
    return jnp.sum(earlier * one_hot, axis=1).reshape(tokens_here, routes)


def on_device(grad_rows, gate_probs, expert_ids, gate_pre, up_pre, down_weight):
    experts_here, rows_here, hidden_width = gate_pre.shape
    feature_width = down_weight.shape[2]
    capacity = CAP
    experts_total = experts_here * lax.axis_size("expert")
    slot_index = slot_table(expert_ids, experts_total)
    first_expert = lax.axis_index("expert") * experts_here
    local_ids = expert_ids - first_expert
    expert_match = (
        local_ids[:, :, None] == jnp.arange(experts_here, dtype=jnp.int32)[None, None, :]
    ).astype(jnp.float32)
    expert_match = expert_match * gate_probs[:, :, None]
    slot_match = (
        slot_index[:, :, None] == jnp.arange(capacity, dtype=jnp.int32)[None, None, :]
    ).astype(jnp.float32)
    placing = jnp.einsum("tke,tks->est", expert_match, slot_match, precision=lax.Precision.HIGHEST)
    dispatched = jnp.einsum(
        "est,td->esd", placing, grad_rows.astype(jnp.float32), precision=lax.Precision.HIGHEST
    ).astype(jnp.bfloat16)
    arrived = lax.all_gather(dispatched, "dp", axis=1, tiled=True)
    gate_value = gate_pre.astype(jnp.float32)
    up_value = up_pre.astype(jnp.float32)
    sigmoid_gate = jax.nn.sigmoid(gate_value)
    silu_gate = gate_value * sigmoid_gate
    hidden = (silu_gate * up_value).astype(jnp.bfloat16)
    partial_sums = jnp.einsum(
        "erd,efd->erf", arrived, down_weight, preferred_element_type=jnp.float32
    )
    own_rows = lax.psum_scatter(
        partial_sums.astype(jnp.bfloat16), "ffn", scatter_dimension=1, tiled=True
    ).astype(jnp.float32)
    gate_grad = (
        own_rows * up_value * sigmoid_gate * (1.0 + gate_value * (1.0 - sigmoid_gate))
    ).astype(jnp.bfloat16)
    up_grad = (own_rows * silu_gate).astype(jnp.bfloat16)
    weight_grad = jnp.einsum(
        "erf,erd->efd",
        lax.all_gather(hidden, "ffn", axis=1, tiled=True),
        arrived,
        preferred_element_type=jnp.float32,
    )
    squares = lax.psum(jnp.sum(weight_grad * weight_grad), ("dp", "expert", "ffn"))
    entry_count = (
        float(experts_total)
        * float(hidden_width * lax.axis_size("dp"))
        * float(feature_width * lax.axis_size("ffn"))
    )
    clip_limit = jnp.float32(0.5 * math.sqrt(entry_count))
    factor = clip_limit / jnp.maximum(jnp.sqrt(squares), clip_limit)
    down_grad = (weight_grad * factor).astype(jnp.bfloat16)
    return (down_grad, gate_grad, up_grad)


def fused_kernel(
    n_dp, meta_ref, rows_ref, gate_ref, up_ref, weight_ref,
    wide_ref, gate_out, up_out, norm_ref,
    tokens, metas, placed, weight, hidden, hidden_t, mine, outgoing, incoming,
    squares, norm_dp, norm_core, norm_pair, own_norm,
    load_sem, meta_send, meta_recv, z_send, z_recv, x_send, x_recv, core_send, core_recv,
    hidden_send, hidden_recv, part_send, part_recv, norm_send, norm_recv, wide_sem,
):
    dp = lax.axis_index("dp")
    core = lax.axis_index("expert")
    side = lax.axis_index("ffn")
    n_z = n_dp // 2
    z, x = dp // 2, dp % 2
    experts, own_slots, units = gate_ref.shape
    block = rows_ref.shape[0]
    half = block // 2
    width = rows_ref.shape[1]
    group = 2 * CAP
    groups_own = n_z // 2

    load_rows = pltpu.make_async_copy(
        rows_ref, tokens.at[z, pl.ds(pl.multiple_of(x * block, block), block), :], load_sem.at[0]
    )
    load_rows.start()
    load_weight = pltpu.make_async_copy(weight_ref, weight, load_sem.at[1])
    load_weight.start()

    barrier = pltpu.get_barrier_semaphore()
    for step in range(1, n_dp):
        pl.semaphore_signal(
            barrier, inc=1, device_id={"dp": (dp + step) % n_dp}, device_id_type=MESH
        )
    pl.semaphore_signal(barrier, inc=1, device_id={"expert": 1 - core}, device_id_type=MESH)
    pl.semaphore_signal(barrier, inc=1, device_id={"ffn": 1 - side}, device_id_type=MESH)
    pl.semaphore_wait(barrier, n_dp + 1)

    def half_rows(z_of, x_of, core_of):
        start = pl.multiple_of(x_of * block + core_of * half, half)
        return tokens.at[z_of, pl.ds(start, half), :]

    def remote(src, dst, send, recv, to):
        return pltpu.make_async_remote_copy(
            src_ref=src, dst_ref=dst, send_sem=send, recv_sem=recv,
            device_id=to, device_id_type=MESH,
        )

    def z_copy(g, up):
        place = half_rows(g, x, core)
        to = jnp.clip(z + (1 if up else -1), 0, n_z - 1) * 2 + x
        return remote(place, place, z_send.at[1 if up else 0, g], z_recv.at[g], {"dp": to})

    def x_copy(g, x_of):
        place = half_rows(g, x_of, core)
        return remote(place, place, x_send.at[g], x_recv.at[g], {"dp": z * 2 + 1 - x})

    def core_copy(g, x_of, core_of):
        place = half_rows(g, x_of, core_of)
        return remote(
            place, place, core_send.at[g, x_of], core_recv.at[g, x_of], {"expert": 1 - core}
        )

    def meta_copy(step, source):
        return remote(
            metas.at[source], metas.at[source], meta_send.at[step], meta_recv.at[step],
            {"dp": (dp + step) % n_dp},
        )

    metas[dp] = meta_ref[...]
    for step in range(1, n_dp):
        meta_copy(step, dp).start()
    load_rows.wait()

    @pl.when(z < n_z - 1)
    def _():
        z_copy(z, True).start()

    @pl.when(z > 0)
    def _():
        z_copy(z, False).start()

    x_copy(z, x).start()

    def hidden_copy(e, side_of):
        start = pl.multiple_of(side_of * own_slots, 16)
        place = hidden.at[e, pl.ds(start, own_slots), :]
        return remote(place, place, hidden_send.at[e], hidden_recv.at[e], {"ffn": 1 - side})

    piece = 48
    for e in range(experts):

        def hidden_piece(i, carry):
            start = pl.multiple_of(i * piece, 16)
            gate = gate_ref[e, pl.ds(start, piece), :].astype(F32)
            up = up_ref[e, pl.ds(start, piece), :].astype(F32)
            to = pl.multiple_of(side * own_slots + start, 16)
            hidden[e, pl.ds(to, piece), :] = (gate * jax.nn.sigmoid(gate) * up).astype(BF16)
            return carry

        lax.fori_loop(0, own_slots // piece, hidden_piece, 0)
        hidden_copy(e, side).start()

    for step in range(1, n_dp):
        meta_copy(step, (dp - step + n_dp) % n_dp).wait_recv()
    load_weight.wait()

    first = (core * experts).astype(F32)
    n_cols = 4
    cols = width // n_cols
    unit_cols = 256

    def part_copy(index, e):
        return remote(
            outgoing.at[index, e], incoming.at[index, e], part_send.at[index, e],
            part_recv.at[index, e], {"ffn": 1 - side},
        )

    def process(g):
        meta = jnp.concatenate([metas[2 * g], metas[2 * g + 1]], axis=1)
        lane = lax.broadcasted_iota(jnp.int32, (2 * block, 2 * block), 1)
        sub = lax.broadcasted_iota(jnp.int32, (2 * block, 2 * block), 0)
        before = jnp.where(
            (sub < lane) & ((sub >= block) == (lane >= block)), 1.0, 0.0
        ).astype(BF16)
        row = lax.broadcasted_iota(jnp.int32, (group, 2 * block), 0).astype(F32)
        offset = jnp.where(
            lax.broadcasted_iota(jnp.int32, (1, 2 * block), 1) >= block, float(CAP), 0.0
        )
        start = pl.multiple_of(g * group, 16)
        for e in range(experts):
            first_match = meta[0:1] == first + e
            second_match = meta[1:2] == first + e
            match = jnp.where(first_match | second_match, 1.0, 0.0)
            prob = jnp.where(first_match, meta[2:3], jnp.where(second_match, meta[3:4], 0.0))
            earlier = jnp.dot(
                jnp.broadcast_to(match, (16, 2 * block)).astype(BF16), before,
                preferred_element_type=F32,
            )[0:1]
            key = jnp.where(match > 0.0, earlier + offset, -1.0)
            chosen = row == key
            scale = jnp.sum(jnp.where(chosen, prob, 0.0), axis=1, keepdims=True)
            select = jnp.where(chosen, 1.0, 0.0).astype(BF16)

            def place_cols(j, carry):
                at = pl.ds(pl.multiple_of(j * cols, 128), cols)
                picked = jnp.dot(select, tokens[g, :, at], preferred_element_type=F32)
                placed[e, pl.ds(start, group), at] = (picked * scale).astype(BF16)
                return carry

            lax.fori_loop(0, n_cols, place_cols, 0)
        is_own = (g // groups_own) == side
        index = g % groups_own
        for e in range(experts):

            def unit_tile(j, carry):
                at = pl.ds(pl.multiple_of(j * unit_cols, 128), unit_cols)
                term = lax.dot_general(
                    placed[e, pl.ds(start, group), :], weight[e, at, :],
                    (((1,), (1,)), ((), ())), preferred_element_type=F32,
                ).astype(BF16)

                @pl.when(is_own)
                def _():
                    mine[index, e, :, at] = term

                @pl.when(jnp.logical_not(is_own))
                def _():
                    outgoing[index, e, :, at] = term

                return carry

            lax.fori_loop(0, units // unit_cols, unit_tile, 0)

            @pl.when(jnp.logical_not(is_own))
            def _():
                part_copy(index, e).start()

    def stage(s, carry):
        for sign in (-1, 1):
            g = z + sign * (s + 1)
            onward = z - sign

            @pl.when((g >= 0) & (g < n_z))
            def _():
                z_copy(g, sign < 0).wait_recv()

                @pl.when((onward >= 0) & (onward < n_z))
                def _():
                    z_copy(g, sign < 0).start()

                x_copy(g, x).start()
                core_copy(g, x, core).start()

        for sign in (-1, 1):
            g = z + sign * s

            @pl.when((g >= 0) & (g < n_z) & ((s > 0) | (sign < 0)))
            def _():
                x_copy(g, 1 - x).wait_recv()
                core_copy(g, 1 - x, core).start()

        def side_of_stage(k, inner):
            g = z + (2 * k - 1) * s

            @pl.when((g >= 0) & (g < n_z) & ((s > 0) | (k == 0)))
            def _():
                @pl.when(s > 0)
                def _():
                    core_copy(g, x, 1 - core).wait_recv()

                core_copy(g, 1 - x, 1 - core).wait_recv()
                process(g)

            return inner

        lax.fori_loop(0, 2, side_of_stage, 0)
        return carry

    lax.fori_loop(0, n_z, stage, 0)

    for e in range(experts):
        hidden_copy(e, 1 - side).wait_recv()
        hidden_copy(e, side).wait_send()
    slots = hidden.shape[1]
    for e in range(experts):

        def turn(j, carry):
            at = pl.ds(pl.multiple_of(j * 128, 128), 128)
            hidden_t[e, at, :] = hidden[e, :, at].T
            return carry

        lax.fori_loop(0, units // 128, turn, 0)

    squares[...] = jnp.zeros_like(squares)
    tile = 256
    tiles = width // tile

    def wide_copy(e, j):
        at = pl.ds(pl.multiple_of(j * tile, 128), tile)
        return pltpu.make_async_copy(weight.at[e, :, at], wide_ref.at[e, :, at], wide_sem.at[e, j])

    for e in range(experts):

        def wide_tile(j, carry):
            at = pl.ds(pl.multiple_of(j * tile, 128), tile)
            product = jnp.dot(hidden_t[e], placed[e, :, at], preferred_element_type=F32)
            weight[e, :, at] = product.astype(BF16)
            squares[...] += jnp.sum((product * product).reshape(units // 8, 8, tile), axis=0)
            wide_copy(e, j).start()
            return carry

        lax.fori_loop(0, tiles, wide_tile, 0)

    own_norm[0] = squares[:, 0:128] + squares[:, 128:256]

    def norm_copy(step, to_slot):
        return remote(
            own_norm.at[0], norm_dp.at[to_slot], norm_send.at[step], norm_recv.at[step],
            {"dp": (dp + step) % n_dp},
        )

    for step in range(1, n_dp):
        norm_copy(step, dp).start()
    norm_dp[dp] = own_norm[0]
    for step in range(1, n_dp):
        norm_copy(step, (dp - step + n_dp) % n_dp).wait_recv()
    total = norm_dp[0]
    for i in range(1, n_dp):
        total = total + norm_dp[i]
    own_norm[1] = total
    core_norm = remote(
        own_norm.at[1], norm_core, norm_send.at[0], norm_recv.at[0], {"expert": 1 - core}
    )
    core_norm.start()
    core_norm.wait()
    own_norm[2] = total + norm_core[...]
    pair_norm = remote(
        own_norm.at[2], norm_pair, norm_send.at[n_dp], norm_recv.at[n_dp], {"ffn": 1 - side}
    )
    pair_norm.start()

    for index in range(groups_own):
        for e in range(experts):
            part_copy(index, e).wait_recv()

            def grad_piece(i, carry):
                here = pl.multiple_of(i * piece, 16)
                at = pl.ds(pl.multiple_of(index * group + here, 16), piece)
                gate = gate_ref[e, at, :].astype(F32)
                up = up_ref[e, at, :].astype(F32)
                grad = (
                    mine[index, e, pl.ds(here, piece), :].astype(F32)
                    + incoming[index, e, pl.ds(here, piece), :].astype(F32)
                )
                sig = jax.nn.sigmoid(gate)
                gate_out[e, at, :] = (grad * up * sig * (1.0 + gate * (1.0 - sig))).astype(BF16)
                up_out[e, at, :] = (grad * (gate * sig)).astype(BF16)
                return carry

            lax.fori_loop(0, group // piece, grad_piece, 0)

    pair_norm.wait()
    norm_ref[...] = own_norm[2] + norm_pair[...]

    for index in range(groups_own):
        for e in range(experts):
            part_copy(index, e).wait_send()
    for step in range(1, n_dp):
        meta_copy(step, dp).wait_send()
        norm_copy(step, dp).wait_send()

    def drain(g, carry):
        @pl.when((z < n_z - 1) & (g <= z))
        def _():
            z_copy(g, True).wait_send()

        @pl.when((z > 0) & (g >= z))
        def _():
            z_copy(g, False).wait_send()

        x_copy(g, x).wait_send()

        @pl.when(g != z)
        def _():
            core_copy(g, x, core).wait_send()

        core_copy(g, 1 - x, core).wait_send()
        return carry

    lax.fori_loop(0, n_z, drain, 0)
    for e in range(experts):

        def wide_wait(j, carry):
            wide_copy(e, j).wait()
            return carry

        lax.fori_loop(0, tiles, wide_wait, 0)


def fused_call(n_dp, meta, grad_rows, gate_pre, up_pre, down_weight):
    experts, own_slots, units = gate_pre.shape
    block, width = grad_rows.shape
    n_z = n_dp // 2
    group = 2 * CAP
    groups_own = n_z // 2
    slots = n_dp * CAP
    vmem = pl.BlockSpec(memory_space=pltpu.VMEM)
    hbm = pl.BlockSpec(memory_space=pl.ANY)
    dma = pltpu.SemaphoreType.DMA
    return pl.pallas_call(
        functools.partial(fused_kernel, n_dp),
        out_shape=(
            jax.ShapeDtypeStruct(down_weight.shape, BF16),
            jax.ShapeDtypeStruct(gate_pre.shape, BF16),
            jax.ShapeDtypeStruct(up_pre.shape, BF16),
            jax.ShapeDtypeStruct((8, 128), F32),
        ),
        in_specs=[vmem, hbm, vmem, vmem, hbm],
        out_specs=(hbm, vmem, vmem, vmem),
        scratch_shapes=[
            pltpu.VMEM((n_z, 2 * block, width), BF16),
            pltpu.VMEM((n_dp, 8, block), F32),
            pltpu.VMEM((experts, slots, width), BF16),
            pltpu.VMEM(down_weight.shape, BF16),
            pltpu.VMEM((experts, slots, units), BF16),
            pltpu.VMEM((experts, units, slots), BF16),
            pltpu.VMEM((groups_own, experts, group, units), BF16),
            pltpu.VMEM((groups_own, experts, group, units), BF16),
            pltpu.VMEM((groups_own, experts, group, units), BF16),
            pltpu.VMEM((8, 256), F32),
            pltpu.VMEM((n_dp, 8, 128), F32),
            pltpu.VMEM((8, 128), F32),
            pltpu.VMEM((8, 128), F32),
            pltpu.VMEM((3, 8, 128), F32),
            dma((2,)),
            dma((n_dp,)),
            dma((n_dp,)),
            dma((2, n_z)),
            dma((n_z,)),
            dma((n_z,)),
            dma((n_z,)),
            dma((n_z, 2)),
            dma((n_z, 2)),
            dma((experts,)),
            dma((experts,)),
            dma((groups_own, experts)),
            dma((groups_own, experts)),
            dma((n_dp + 1,)),
            dma((n_dp + 1,)),
            dma((experts, width // 256)),
        ],
        compiler_params=pltpu.CompilerParams(
            collective_id=0, has_side_effects=True, vmem_limit_bytes=58 * 1024 * 1024
        ),
    )(meta, grad_rows, gate_pre, up_pre, down_weight)


def fused_device(grad_rows, gate_probs, expert_ids, gate_pre, up_pre, down_weight):
    experts_here, rows_here, hidden_width = gate_pre.shape
    feature_width = down_weight.shape[2]
    n_dp = lax.axis_size("dp")
    meta = jnp.concatenate(
        [expert_ids.astype(F32), gate_probs, jnp.zeros((expert_ids.shape[0], 4), F32)], axis=1
    ).T
    wide, gate_grad, up_grad, norm = fused_call(
        n_dp, meta, grad_rows, gate_pre, up_pre, down_weight
    )
    squares = jnp.sum(norm)
    entry_count = (
        float(experts_here * lax.axis_size("expert"))
        * float(hidden_width * n_dp)
        * float(feature_width * lax.axis_size("ffn"))
    )
    clip_limit = jnp.float32(0.5 * math.sqrt(entry_count))
    factor = clip_limit / jnp.maximum(jnp.sqrt(squares), clip_limit)
    down_grad = (wide.astype(F32) * factor).astype(BF16)
    return (down_grad, gate_grad, up_grad)


def solution(mesh):
    placed = (
        P("dp", "ffn"),
        P("dp", None),
        P("dp", None),
        P("expert", "ffn", "dp"),
        P("expert", "ffn", "dp"),
        P("expert", "dp", "ffn"),
    )
    fits = mesh.shape["dp"] == 8 and mesh.shape["expert"] == 2 and mesh.shape["ffn"] == 2
    return jax.shard_map(
        fused_device if fits else on_device,
        mesh=mesh,
        in_specs=placed,
        out_specs=(P("expert", "dp", "ffn"), P("expert", "ffn", "dp"), P("expert", "ffn", "dp")),
        check_vma=False,
    )
```

```python
import functools
import math

import jax
import jax.numpy as jnp
from jax import lax
from jax.experimental import pallas as pl
from jax.experimental.pallas import tpu as pltpu
from jax.sharding import PartitionSpec as P

CAP = 72
MESH = pl.DeviceIdType.MESH
F32 = jnp.float32
BF16 = jnp.bfloat16


def slot_table(route_ids, experts_total):
    tokens_here, routes = route_ids.shape
    flat_ids = route_ids.reshape(tokens_here * routes)
    one_hot = (flat_ids[:, None] == jnp.arange(experts_total, dtype=jnp.int32)[None, :]).astype(
        jnp.int32
    )
    earlier = jnp.cumsum(one_hot, axis=0) - one_hot
    return jnp.sum(earlier * one_hot, axis=1).reshape(tokens_here, routes)


def on_device(grad_rows, gate_probs, expert_ids, gate_pre, up_pre, down_weight):
    experts_here, rows_here, hidden_width = gate_pre.shape
    feature_width = down_weight.shape[2]
    capacity = CAP
    experts_total = experts_here * lax.axis_size("expert")
    slot_index = slot_table(expert_ids, experts_total)
    first_expert = lax.axis_index("expert") * experts_here
    local_ids = expert_ids - first_expert
    expert_match = (
        local_ids[:, :, None] == jnp.arange(experts_here, dtype=jnp.int32)[None, None, :]
    ).astype(jnp.float32)
    expert_match = expert_match * gate_probs[:, :, None]
    slot_match = (
        slot_index[:, :, None] == jnp.arange(capacity, dtype=jnp.int32)[None, None, :]
    ).astype(jnp.float32)
    placing = jnp.einsum("tke,tks->est", expert_match, slot_match, precision=lax.Precision.HIGHEST)
    dispatched = jnp.einsum(
        "est,td->esd", placing, grad_rows.astype(jnp.float32), precision=lax.Precision.HIGHEST
    ).astype(jnp.bfloat16)
    arrived = lax.all_gather(dispatched, "dp", axis=1, tiled=True)
    gate_value = gate_pre.astype(jnp.float32)
    up_value = up_pre.astype(jnp.float32)
    sigmoid_gate = jax.nn.sigmoid(gate_value)
    silu_gate = gate_value * sigmoid_gate
    hidden = (silu_gate * up_value).astype(jnp.bfloat16)
    partial_sums = jnp.einsum(
        "erd,efd->erf", arrived, down_weight, preferred_element_type=jnp.float32
    )
    own_rows = lax.psum_scatter(
        partial_sums.astype(jnp.bfloat16), "ffn", scatter_dimension=1, tiled=True
    ).astype(jnp.float32)
    gate_grad = (
        own_rows * up_value * sigmoid_gate * (1.0 + gate_value * (1.0 - sigmoid_gate))
    ).astype(jnp.bfloat16)
    up_grad = (own_rows * silu_gate).astype(jnp.bfloat16)
    weight_grad = jnp.einsum(
        "erf,erd->efd",
        lax.all_gather(hidden, "ffn", axis=1, tiled=True),
        arrived,
        preferred_element_type=jnp.float32,
    )
    squares = lax.psum(jnp.sum(weight_grad * weight_grad), ("dp", "expert", "ffn"))
    entry_count = (
        float(experts_total)
        * float(hidden_width * lax.axis_size("dp"))
        * float(feature_width * lax.axis_size("ffn"))
    )
    clip_limit = jnp.float32(0.5 * math.sqrt(entry_count))
    factor = clip_limit / jnp.maximum(jnp.sqrt(squares), clip_limit)
    down_grad = (weight_grad * factor).astype(jnp.bfloat16)
    return (down_grad, gate_grad, up_grad)


def fused_kernel(
    n_dp, ids_ref, probs_ref, rows_ref, gate_ref, up_ref, weight_ref,
    placed_out, hidden_out, mine_out, incoming, norm_ref,
    tokens, metas, placed, weight, hidden, hidden_t, mine, outgoing,
    squares, norm_dp, norm_core, norm_pair, own_norm,
    load_sem, meta_send, meta_recv, z_send, z_recv, x_send, x_recv, core_send, core_recv,
    hidden_send, hidden_recv, part_send, part_recv, norm_send, norm_recv, store_sem,
):
    dp = lax.axis_index("dp")
    core = lax.axis_index("expert")
    side = lax.axis_index("ffn")
    n_z = n_dp // 2
    z, x = dp // 2, dp % 2
    experts, own_slots, units = gate_ref.shape
    block = rows_ref.shape[0]
    half = block // 2
    width = rows_ref.shape[1]
    group = 2 * CAP
    groups_own = n_z // 2

    load_rows = pltpu.make_async_copy(
        rows_ref, tokens.at[z, pl.ds(pl.multiple_of(x * block, block), block), :], load_sem.at[0]
    )
    load_rows.start()
    load_weight = pltpu.make_async_copy(weight_ref, weight, load_sem.at[1])
    load_weight.start()

    barrier = pltpu.get_barrier_semaphore()
    for step in range(1, n_dp):
        pl.semaphore_signal(
            barrier, inc=1, device_id={"dp": (dp + step) % n_dp}, device_id_type=MESH
        )
    pl.semaphore_signal(barrier, inc=1, device_id={"expert": 1 - core}, device_id_type=MESH)
    pl.semaphore_signal(barrier, inc=1, device_id={"ffn": 1 - side}, device_id_type=MESH)
    pl.semaphore_wait(barrier, n_dp + 1)

    def half_rows(z_of, x_of, core_of):
        start = pl.multiple_of(x_of * block + core_of * half, half)
        return tokens.at[z_of, pl.ds(start, half), :]

    def remote(src, dst, send, recv, to):
        return pltpu.make_async_remote_copy(
            src_ref=src, dst_ref=dst, send_sem=send, recv_sem=recv,
            device_id=to, device_id_type=MESH,
        )

    def z_copy(g, up):
        place = half_rows(g, x, core)
        to = jnp.clip(z + (1 if up else -1), 0, n_z - 1) * 2 + x
        return remote(place, place, z_send.at[1 if up else 0, g], z_recv.at[g], {"dp": to})

    def x_copy(g, x_of):
        place = half_rows(g, x_of, core)
        return remote(place, place, x_send.at[g], x_recv.at[g], {"dp": z * 2 + 1 - x})

    def core_copy(g, x_of, core_of):
        place = half_rows(g, x_of, core_of)
        return remote(
            place, place, core_send.at[g, x_of], core_recv.at[g, x_of], {"expert": 1 - core}
        )

    def meta_copy(step, source):
        return remote(
            metas.at[source], metas.at[source], meta_send.at[step], meta_recv.at[step],
            {"dp": (dp + step) % n_dp},
        )

    metas[dp] = jnp.concatenate(
        [ids_ref[...].astype(F32), probs_ref[...], jnp.zeros((4, block), F32)], axis=0
    )
    for step in range(1, n_dp):
        meta_copy(step, dp).start()
    load_rows.wait()

    @pl.when(z < n_z - 1)
    def _():
        z_copy(z, True).start()

    @pl.when(z > 0)
    def _():
        z_copy(z, False).start()

    x_copy(z, x).start()

    def hidden_copy(e, side_of):
        start = pl.multiple_of(side_of * own_slots, 16)
        place = hidden.at[e, pl.ds(start, own_slots), :]
        return remote(place, place, hidden_send.at[e], hidden_recv.at[e], {"ffn": 1 - side})

    piece = 48
    for e in range(experts):

        def hidden_piece(i, carry):
            start = pl.multiple_of(i * piece, 16)
            gate = gate_ref[e, pl.ds(start, piece), :].astype(F32)
            up = up_ref[e, pl.ds(start, piece), :].astype(F32)
            to = pl.multiple_of(side * own_slots + start, 16)
            hidden[e, pl.ds(to, piece), :] = (gate * jax.nn.sigmoid(gate) * up).astype(BF16)
            return carry

        lax.fori_loop(0, own_slots // piece, hidden_piece, 0)
        hidden_copy(e, side).start()

    for step in range(1, n_dp):
        meta_copy(step, (dp - step + n_dp) % n_dp).wait_recv()
    load_weight.wait()

    first = (core * experts).astype(F32)
    n_cols = 4
    cols = width // n_cols
    unit_cols = 256

    def part_copy(index, e):
        at = pl.ds(pl.multiple_of(index * group, 16), group)
        return remote(
            outgoing.at[e, at, :], incoming.at[e, at, :], part_send.at[index, e],
            part_recv.at[index, e], {"ffn": 1 - side},
        )

    def process(g):
        meta = jnp.concatenate([metas[2 * g], metas[2 * g + 1]], axis=1)
        lane = lax.broadcasted_iota(jnp.int32, (2 * block, 2 * block), 1)
        sub = lax.broadcasted_iota(jnp.int32, (2 * block, 2 * block), 0)
        before = jnp.where(
            (sub < lane) & ((sub >= block) == (lane >= block)), 1.0, 0.0
        ).astype(BF16)
        row = lax.broadcasted_iota(jnp.int32, (group, 2 * block), 0).astype(F32)
        offset = jnp.where(
            lax.broadcasted_iota(jnp.int32, (1, 2 * block), 1) >= block, float(CAP), 0.0
        )
        start = pl.multiple_of(g * group, 16)
        for e in range(experts):
            first_match = meta[0:1] == first + e
            second_match = meta[1:2] == first + e
            match = jnp.where(first_match | second_match, 1.0, 0.0)
            prob = jnp.where(first_match, meta[2:3], jnp.where(second_match, meta[3:4], 0.0))
            earlier = jnp.dot(
                jnp.broadcast_to(match, (16, 2 * block)).astype(BF16), before,
                preferred_element_type=F32,
            )[0:1]
            key = jnp.where(match > 0.0, earlier + offset, -1.0)
            chosen = row == key
            scale = jnp.sum(jnp.where(chosen, prob, 0.0), axis=1, keepdims=True)
            select = jnp.where(chosen, 1.0, 0.0).astype(BF16)

            def place_cols(j, carry):
                at = pl.ds(pl.multiple_of(j * cols, 128), cols)
                picked = jnp.dot(select, tokens[g, :, at], preferred_element_type=F32)
                placed[e, pl.ds(start, group), at] = (picked * scale).astype(BF16)
                return carry

            lax.fori_loop(0, n_cols, place_cols, 0)
        is_own = (g // groups_own) == side
        index = g % groups_own
        index_rows = pl.ds(pl.multiple_of(index * group, 16), group)
        for e in range(experts):

            def unit_tile(j, carry):
                at = pl.ds(pl.multiple_of(j * unit_cols, 128), unit_cols)
                term = lax.dot_general(
                    placed[e, pl.ds(start, group), :], weight[e, at, :],
                    (((1,), (1,)), ((), ())), preferred_element_type=F32,
                ).astype(BF16)

                @pl.when(is_own)
                def _():
                    mine[e, index_rows, at] = term

                @pl.when(jnp.logical_not(is_own))
                def _():
                    outgoing[e, index_rows, at] = term

                return carry

            lax.fori_loop(0, units // unit_cols, unit_tile, 0)

            @pl.when(jnp.logical_not(is_own))
            def _():
                part_copy(index, e).start()

    def stage(s, carry):
        for sign in (-1, 1):
            g = z + sign * (s + 1)
            onward = z - sign

            @pl.when((g >= 0) & (g < n_z))
            def _():
                z_copy(g, sign < 0).wait_recv()

                @pl.when((onward >= 0) & (onward < n_z))
                def _():
                    z_copy(g, sign < 0).start()

                x_copy(g, x).start()
                core_copy(g, x, core).start()

        for sign in (-1, 1):
            g = z + sign * s

            @pl.when((g >= 0) & (g < n_z) & ((s > 0) | (sign < 0)))
            def _():
                x_copy(g, 1 - x).wait_recv()
                core_copy(g, 1 - x, core).start()

        def side_of_stage(k, inner):
            g = z + (2 * k - 1) * s

            @pl.when((g >= 0) & (g < n_z) & ((s > 0) | (k == 0)))
            def _():
                @pl.when(s > 0)
                def _():
                    core_copy(g, x, 1 - core).wait_recv()

                core_copy(g, 1 - x, 1 - core).wait_recv()
                process(g)

            return inner

        lax.fori_loop(0, 2, side_of_stage, 0)
        return carry

    lax.fori_loop(0, n_z, stage, 0)

    store_placed = pltpu.make_async_copy(placed, placed_out, store_sem.at[0])
    store_placed.start()
    store_mine = pltpu.make_async_copy(mine, mine_out, store_sem.at[1])
    store_mine.start()
    for e in range(experts):
        hidden_copy(e, 1 - side).wait_recv()
        hidden_copy(e, side).wait_send()

    squares[...] = jnp.zeros_like(squares)
    slots = hidden.shape[1]
    part = slots // 2
    contract = (((1,), (1,)), ((), ()))

    def add_squares(e, carry):
        for a, b in ((0, 0), (0, 1), (1, 1)):
            left, right = pl.ds(a * part, part), pl.ds(b * part, part)
            rows_product = lax.dot_general(
                placed[e, left, :], placed[e, right, :], contract, preferred_element_type=F32
            )
            hidden_product = lax.dot_general(
                hidden[e, left, :], hidden[e, right, :], contract, preferred_element_type=F32
            )
            both = rows_product * hidden_product
            if a != b:
                both = both + both
            folded = jnp.sum(both.reshape(part // 8, 8, part), axis=0)
            squares[...] += jnp.broadcast_to(jnp.sum(folded, axis=1, keepdims=True), (8, 128))
        return carry

    lax.fori_loop(0, experts, add_squares, 0)

    own_norm[0] = squares[...]

    def norm_copy(step, to_slot):
        return remote(
            own_norm.at[0], norm_dp.at[to_slot], norm_send.at[step], norm_recv.at[step],
            {"dp": (dp + step) % n_dp},
        )

    for step in range(1, n_dp):
        norm_copy(step, dp).start()
    norm_dp[dp] = own_norm[0]
    for e in range(experts):

        def turn(j, carry):
            at = pl.ds(pl.multiple_of(j * 128, 128), 128)
            hidden_t[e, at, :] = hidden[e, :, at].T
            return carry

        lax.fori_loop(0, units // 128, turn, 0)
    store_hidden = pltpu.make_async_copy(hidden_t, hidden_out, store_sem.at[2])
    store_hidden.start()
    for step in range(1, n_dp):
        norm_copy(step, (dp - step + n_dp) % n_dp).wait_recv()
    total = norm_dp[0]
    for i in range(1, n_dp):
        total = total + norm_dp[i]
    own_norm[1] = total
    core_norm = remote(
        own_norm.at[1], norm_core, norm_send.at[0], norm_recv.at[0], {"expert": 1 - core}
    )
    core_norm.start()
    core_norm.wait()
    own_norm[2] = total + norm_core[...]
    pair_norm = remote(
        own_norm.at[2], norm_pair, norm_send.at[n_dp], norm_recv.at[n_dp], {"ffn": 1 - side}
    )
    pair_norm.start()

    pair_norm.wait()
    norm_ref[...] = own_norm[2] + norm_pair[...]

    for index in range(groups_own):
        for e in range(experts):
            part_copy(index, e).wait()
    for step in range(1, n_dp):
        meta_copy(step, dp).wait_send()
        norm_copy(step, dp).wait_send()

    def drain(g, carry):
        @pl.when((z < n_z - 1) & (g <= z))
        def _():
            z_copy(g, True).wait_send()

        @pl.when((z > 0) & (g >= z))
        def _():
            z_copy(g, False).wait_send()

        x_copy(g, x).wait_send()

        @pl.when(g != z)
        def _():
            core_copy(g, x, core).wait_send()

        core_copy(g, 1 - x, core).wait_send()
        return carry

    lax.fori_loop(0, n_z, drain, 0)
    store_placed.wait()
    store_mine.wait()
    store_hidden.wait()


def fused_call(n_dp, ids, probs, grad_rows, gate_pre, up_pre, down_weight):
    experts, own_slots, units = gate_pre.shape
    block, width = grad_rows.shape
    n_z = n_dp // 2
    groups_own = n_z // 2
    slots = n_dp * CAP
    vmem = pl.BlockSpec(memory_space=pltpu.VMEM)
    hbm = pl.BlockSpec(memory_space=pl.ANY)
    dma = pltpu.SemaphoreType.DMA
    return pl.pallas_call(
        functools.partial(fused_kernel, n_dp),
        out_shape=(
            jax.ShapeDtypeStruct((experts, slots, width), BF16),
            jax.ShapeDtypeStruct((experts, units, slots), BF16),
            jax.ShapeDtypeStruct(gate_pre.shape, BF16),
            jax.ShapeDtypeStruct(gate_pre.shape, BF16),
            jax.ShapeDtypeStruct((8, 128), F32),
        ),
        in_specs=[vmem, vmem, hbm, vmem, vmem, hbm],
        out_specs=(hbm, hbm, hbm, hbm, vmem),
        scratch_shapes=[
            pltpu.VMEM((n_z, 2 * block, width), BF16),
            pltpu.VMEM((n_dp, 8, block), F32),
            pltpu.VMEM((experts, slots, width), BF16),
            pltpu.VMEM(down_weight.shape, BF16),
            pltpu.VMEM((experts, slots, units), BF16),
            pltpu.VMEM((experts, units, slots), BF16),
            pltpu.VMEM(gate_pre.shape, BF16),
            pltpu.VMEM(gate_pre.shape, BF16),
            pltpu.VMEM((8, 128), F32),
            pltpu.VMEM((n_dp, 8, 128), F32),
            pltpu.VMEM((8, 128), F32),
            pltpu.VMEM((8, 128), F32),
            pltpu.VMEM((3, 8, 128), F32),
            dma((2,)),
            dma((n_dp,)),
            dma((n_dp,)),
            dma((2, n_z)),
            dma((n_z,)),
            dma((n_z,)),
            dma((n_z,)),
            dma((n_z, 2)),
            dma((n_z, 2)),
            dma((experts,)),
            dma((experts,)),
            dma((groups_own, experts)),
            dma((groups_own, experts)),
            dma((n_dp + 1,)),
            dma((n_dp + 1,)),
            dma((3,)),
        ],
        compiler_params=pltpu.CompilerParams(
            collective_id=0, has_side_effects=True, vmem_limit_bytes=58 * 1024 * 1024
        ),
    )(ids, probs, grad_rows, gate_pre, up_pre, down_weight)


def finish_kernel(
    clip_limit, norm_ref, hidden_ref, placed_ref, gate_ref, up_ref, mine_ref, theirs_ref,
    wide_out, gate_out, up_out,
):
    squares = jnp.sum(jnp.sum(norm_ref[...], axis=0, keepdims=True), axis=1, keepdims=True) / 128.0
    factor = clip_limit / jnp.maximum(jnp.sqrt(squares), clip_limit)
    product = jnp.dot(hidden_ref[0], placed_ref[0], preferred_element_type=F32)
    wide_out[0] = (product * factor).astype(BF16)
    gate = gate_ref[0].astype(F32)
    up = up_ref[0].astype(F32)
    grad = mine_ref[0].astype(F32) + theirs_ref[0].astype(F32)
    sig = jax.nn.sigmoid(gate)
    gate_out[0] = (grad * up * sig * (1.0 + gate * (1.0 - sig))).astype(BF16)
    up_out[0] = (grad * (gate * sig)).astype(BF16)


def finish_call(clip_limit, norm, hidden_t, placed, gate_pre, up_pre, mine, theirs):
    experts, units, slots = hidden_t.shape
    width = placed.shape[2]
    steps = 6
    tile, piece = width // steps, gate_pre.shape[1] // steps
    rows = pl.BlockSpec((1, piece, units), lambda e, j: (e, j, 0))
    return pl.pallas_call(
        functools.partial(finish_kernel, clip_limit),
        grid=(experts, steps),
        out_shape=(
            jax.ShapeDtypeStruct((experts, units, width), BF16),
            jax.ShapeDtypeStruct(gate_pre.shape, BF16),
            jax.ShapeDtypeStruct(gate_pre.shape, BF16),
        ),
        in_specs=[
            pl.BlockSpec((8, 128), lambda e, j: (0, 0)),
            pl.BlockSpec((1, units, slots), lambda e, j: (e, 0, 0)),
            pl.BlockSpec((1, slots, tile), lambda e, j: (e, 0, j)),
            rows, rows, rows, rows,
        ],
        out_specs=(pl.BlockSpec((1, units, tile), lambda e, j: (e, 0, j)), rows, rows),
        compiler_params=pltpu.CompilerParams(vmem_limit_bytes=60 * 1024 * 1024),
    )(norm, hidden_t, placed, gate_pre, up_pre, mine, theirs)


def fused_device(grad_rows, gate_probs, expert_ids, gate_pre, up_pre, down_weight):
    n_dp = lax.axis_size("dp")
    entry_count = (
        float(gate_pre.shape[0] * lax.axis_size("expert"))
        * float(gate_pre.shape[2] * n_dp)
        * float(down_weight.shape[2] * lax.axis_size("ffn"))
    )
    clip_limit = 0.5 * math.sqrt(entry_count)
    placed, hidden_t, mine, theirs, norm = fused_call(
        n_dp, expert_ids.T, gate_probs.T, grad_rows, gate_pre, up_pre, down_weight
    )
    return finish_call(clip_limit, norm, hidden_t, placed, gate_pre, up_pre, mine, theirs)


def solution(mesh):
    placed = (
        P("dp", "ffn"),
        P("dp", None),
        P("dp", None),
        P("expert", "ffn", "dp"),
        P("expert", "ffn", "dp"),
        P("expert", "dp", "ffn"),
    )
    fits = mesh.shape["dp"] == 8 and mesh.shape["expert"] == 2 and mesh.shape["ffn"] == 2
    return jax.shard_map(
        fused_device if fits else on_device,
        mesh=mesh,
        in_specs=placed,
        out_specs=(P("expert", "dp", "ffn"), P("expert", "ffn", "dp"), P("expert", "ffn", "dp")),
        check_vma=False,
    )
```

```python
import functools
import math

import jax
import jax.numpy as jnp
from jax import lax
from jax.experimental import pallas as pl
from jax.experimental.pallas import tpu as pltpu
from jax.sharding import PartitionSpec as P

CAP = 72
MESH = pl.DeviceIdType.MESH
F32 = jnp.float32
BF16 = jnp.bfloat16


def slot_table(route_ids, experts_total):
    tokens_here, routes = route_ids.shape
    flat_ids = route_ids.reshape(tokens_here * routes)
    one_hot = (flat_ids[:, None] == jnp.arange(experts_total, dtype=jnp.int32)[None, :]).astype(
        jnp.int32
    )
    earlier = jnp.cumsum(one_hot, axis=0) - one_hot
    return jnp.sum(earlier * one_hot, axis=1).reshape(tokens_here, routes)


def on_device(grad_rows, gate_probs, expert_ids, gate_pre, up_pre, down_weight):
    experts_here, rows_here, hidden_width = gate_pre.shape
    feature_width = down_weight.shape[2]
    capacity = CAP
    experts_total = experts_here * lax.axis_size("expert")
    slot_index = slot_table(expert_ids, experts_total)
    first_expert = lax.axis_index("expert") * experts_here
    local_ids = expert_ids - first_expert
    expert_match = (
        local_ids[:, :, None] == jnp.arange(experts_here, dtype=jnp.int32)[None, None, :]
    ).astype(jnp.float32)
    expert_match = expert_match * gate_probs[:, :, None]
    slot_match = (
        slot_index[:, :, None] == jnp.arange(capacity, dtype=jnp.int32)[None, None, :]
    ).astype(jnp.float32)
    placing = jnp.einsum("tke,tks->est", expert_match, slot_match, precision=lax.Precision.HIGHEST)
    dispatched = jnp.einsum(
        "est,td->esd", placing, grad_rows.astype(jnp.float32), precision=lax.Precision.HIGHEST
    ).astype(jnp.bfloat16)
    arrived = lax.all_gather(dispatched, "dp", axis=1, tiled=True)
    gate_value = gate_pre.astype(jnp.float32)
    up_value = up_pre.astype(jnp.float32)
    sigmoid_gate = jax.nn.sigmoid(gate_value)
    silu_gate = gate_value * sigmoid_gate
    hidden = (silu_gate * up_value).astype(jnp.bfloat16)
    partial_sums = jnp.einsum(
        "erd,efd->erf", arrived, down_weight, preferred_element_type=jnp.float32
    )
    own_rows = lax.psum_scatter(
        partial_sums.astype(jnp.bfloat16), "ffn", scatter_dimension=1, tiled=True
    ).astype(jnp.float32)
    gate_grad = (
        own_rows * up_value * sigmoid_gate * (1.0 + gate_value * (1.0 - sigmoid_gate))
    ).astype(jnp.bfloat16)
    up_grad = (own_rows * silu_gate).astype(jnp.bfloat16)
    weight_grad = jnp.einsum(
        "erf,erd->efd",
        lax.all_gather(hidden, "ffn", axis=1, tiled=True),
        arrived,
        preferred_element_type=jnp.float32,
    )
    squares = lax.psum(jnp.sum(weight_grad * weight_grad), ("dp", "expert", "ffn"))
    entry_count = (
        float(experts_total)
        * float(hidden_width * lax.axis_size("dp"))
        * float(feature_width * lax.axis_size("ffn"))
    )
    clip_limit = jnp.float32(0.5 * math.sqrt(entry_count))
    factor = clip_limit / jnp.maximum(jnp.sqrt(squares), clip_limit)
    down_grad = (weight_grad * factor).astype(jnp.bfloat16)
    return (down_grad, gate_grad, up_grad)


def fused_kernel(
    n_dp, ids_ref, probs_ref, rows_ref, gate_ref, up_ref, weight_ref,
    placed, hidden_t, mine, incoming, norm_ref,
    tokens, metas, weight, hidden, outgoing,
    squares, norm_dp, norm_core, norm_pair, own_norm,
    load_sem, meta_send, meta_recv, z_send, z_recv, x_send, x_recv, core_send, core_recv,
    hidden_send, hidden_recv, part_send, part_recv, norm_send, norm_recv,
):
    dp = lax.axis_index("dp")
    core = lax.axis_index("expert")
    side = lax.axis_index("ffn")
    n_z = n_dp // 2
    z, x = dp // 2, dp % 2
    experts, own_slots, units = gate_ref.shape
    block = rows_ref.shape[0]
    half = block // 2
    width = rows_ref.shape[1]
    group = 2 * CAP
    groups_own = n_z // 2

    load_rows = pltpu.make_async_copy(
        rows_ref, tokens.at[z, pl.ds(pl.multiple_of(x * block, block), block), :], load_sem.at[0]
    )
    load_rows.start()
    load_weight = pltpu.make_async_copy(weight_ref, weight, load_sem.at[1])
    load_weight.start()

    barrier = pltpu.get_barrier_semaphore()
    for step in range(1, n_dp):
        pl.semaphore_signal(
            barrier, inc=1, device_id={"dp": (dp + step) % n_dp}, device_id_type=MESH
        )
    pl.semaphore_signal(barrier, inc=1, device_id={"expert": 1 - core}, device_id_type=MESH)
    pl.semaphore_signal(barrier, inc=1, device_id={"ffn": 1 - side}, device_id_type=MESH)
    piece = 48

    def make_hidden(e):
        def hidden_piece(i, carry):
            start = pl.multiple_of(i * piece, 16)
            gate = gate_ref[e, pl.ds(start, piece), :].astype(F32)
            up = up_ref[e, pl.ds(start, piece), :].astype(F32)
            to = pl.multiple_of(side * own_slots + start, 16)
            hidden[e, pl.ds(to, piece), :] = (gate * jax.nn.sigmoid(gate) * up).astype(BF16)
            return carry

        lax.fori_loop(0, own_slots // piece, hidden_piece, 0)

    make_hidden(0)
    pl.semaphore_wait(barrier, n_dp + 1)

    def half_rows(z_of, x_of, core_of):
        start = pl.multiple_of(x_of * block + core_of * half, half)
        return tokens.at[z_of, pl.ds(start, half), :]

    def remote(src, dst, send, recv, to):
        return pltpu.make_async_remote_copy(
            src_ref=src, dst_ref=dst, send_sem=send, recv_sem=recv,
            device_id=to, device_id_type=MESH,
        )

    def z_copy(g, up):
        place = half_rows(g, x, core)
        to = jnp.clip(z + (1 if up else -1), 0, n_z - 1) * 2 + x
        return remote(place, place, z_send.at[1 if up else 0, g], z_recv.at[g], {"dp": to})

    def x_copy(g, x_of):
        place = half_rows(g, x_of, core)
        return remote(place, place, x_send.at[g], x_recv.at[g], {"dp": z * 2 + 1 - x})

    def core_copy(g, x_of, core_of):
        place = half_rows(g, x_of, core_of)
        return remote(
            place, place, core_send.at[g, x_of], core_recv.at[g, x_of], {"expert": 1 - core}
        )

    def meta_copy(step, source):
        return remote(
            metas.at[source], metas.at[source], meta_send.at[step], meta_recv.at[step],
            {"dp": (dp + step) % n_dp},
        )

    metas[dp] = jnp.concatenate(
        [ids_ref[...].astype(F32), probs_ref[...], jnp.zeros((4, block), F32)], axis=0
    )
    for step in range(1, n_dp):
        meta_copy(step, dp).start()
    load_rows.wait()

    @pl.when(z < n_z - 1)
    def _():
        z_copy(z, True).start()

    @pl.when(z > 0)
    def _():
        z_copy(z, False).start()

    x_copy(z, x).start()

    def hidden_copy(e, side_of):
        start = pl.multiple_of(side_of * own_slots, 16)
        place = hidden.at[e, pl.ds(start, own_slots), :]
        return remote(place, place, hidden_send.at[e], hidden_recv.at[e], {"ffn": 1 - side})

    hidden_copy(0, side).start()
    for e in range(1, experts):
        make_hidden(e)
        hidden_copy(e, side).start()

    for step in range(1, n_dp):
        meta_copy(step, (dp - step + n_dp) % n_dp).wait_recv()
    load_weight.wait()

    first = (core * experts).astype(F32)
    n_cols = 4
    cols = width // n_cols
    unit_cols = 256

    def part_copy(index, e):
        at = pl.ds(pl.multiple_of(index * group, 16), group)
        return remote(
            outgoing.at[e, at, :], incoming.at[e, at, :], part_send.at[index, e],
            part_recv.at[index, e], {"ffn": 1 - side},
        )

    def process(g):
        meta = jnp.concatenate([metas[2 * g], metas[2 * g + 1]], axis=1)
        lane = lax.broadcasted_iota(jnp.int32, (2 * block, 2 * block), 1)
        sub = lax.broadcasted_iota(jnp.int32, (2 * block, 2 * block), 0)
        before = jnp.where(
            (sub < lane) & ((sub >= block) == (lane >= block)), 1.0, 0.0
        ).astype(BF16)
        row = lax.broadcasted_iota(jnp.int32, (group, 2 * block), 0).astype(F32)
        offset = jnp.where(
            lax.broadcasted_iota(jnp.int32, (1, 2 * block), 1) >= block, float(CAP), 0.0
        )
        start = pl.multiple_of(g * group, 16)
        for e in range(experts):
            first_match = meta[0:1] == first + e
            second_match = meta[1:2] == first + e
            match = jnp.where(first_match | second_match, 1.0, 0.0)
            prob = jnp.where(first_match, meta[2:3], jnp.where(second_match, meta[3:4], 0.0))
            earlier = jnp.dot(
                jnp.broadcast_to(match, (16, 2 * block)).astype(BF16), before,
                preferred_element_type=F32,
            )[0:1]
            key = jnp.where(match > 0.0, earlier + offset, -1.0)
            chosen = row == key
            scale = jnp.sum(jnp.where(chosen, prob, 0.0), axis=1, keepdims=True)
            select = jnp.where(chosen, 1.0, 0.0).astype(BF16)

            def place_cols(j, carry):
                at = pl.ds(pl.multiple_of(j * cols, 128), cols)
                picked = jnp.dot(select, tokens[g, :, at], preferred_element_type=F32)
                placed[e, pl.ds(start, group), at] = (picked * scale).astype(BF16)
                return carry

            lax.fori_loop(0, n_cols, place_cols, 0)
        is_own = (g // groups_own) == side
        index = g % groups_own
        index_rows = pl.ds(pl.multiple_of(index * group, 16), group)
        for e in range(experts):

            def unit_tile(j, carry):
                at = pl.ds(pl.multiple_of(j * unit_cols, 128), unit_cols)
                term = lax.dot_general(
                    placed[e, pl.ds(start, group), :], weight[e, at, :],
                    (((1,), (1,)), ((), ())), preferred_element_type=F32,
                ).astype(BF16)

                @pl.when(is_own)
                def _():
                    mine[e, index_rows, at] = term

                @pl.when(jnp.logical_not(is_own))
                def _():
                    outgoing[e, index_rows, at] = term

                return carry

            lax.fori_loop(0, units // unit_cols, unit_tile, 0)

            @pl.when(jnp.logical_not(is_own))
            def _():
                part_copy(index, e).start()

    def stage(s, carry):
        for sign in (-1, 1):
            g = z + sign * (s + 1)
            onward = z - sign

            @pl.when((g >= 0) & (g < n_z))
            def _():
                z_copy(g, sign < 0).wait_recv()

                @pl.when((onward >= 0) & (onward < n_z))
                def _():
                    z_copy(g, sign < 0).start()

                x_copy(g, x).start()
                core_copy(g, x, core).start()

        for sign in (-1, 1):
            g = z + sign * s

            @pl.when((g >= 0) & (g < n_z) & ((s > 0) | (sign < 0)))
            def _():
                x_copy(g, 1 - x).wait_recv()
                core_copy(g, 1 - x, core).start()

        def side_of_stage(k, inner):
            g = z + (2 * k - 1) * s

            @pl.when((g >= 0) & (g < n_z) & ((s > 0) | (k == 0)))
            def _():
                @pl.when(s > 0)
                def _():
                    core_copy(g, x, 1 - core).wait_recv()

                core_copy(g, 1 - x, 1 - core).wait_recv()
                process(g)

            return inner

        lax.fori_loop(0, 2, side_of_stage, 0)
        return carry

    lax.fori_loop(0, n_z, stage, 0)

    for e in range(experts):
        hidden_copy(e, 1 - side).wait_recv()
        hidden_copy(e, side).wait_send()

    squares[...] = jnp.zeros_like(squares)
    slots = hidden.shape[1]
    part = slots // 2
    contract = (((1,), (1,)), ((), ()))

    def add_squares(e, carry):
        for a, b in ((0, 0), (0, 1), (1, 1)):
            left, right = pl.ds(a * part, part), pl.ds(b * part, part)
            rows_product = lax.dot_general(
                placed[e, left, :], placed[e, right, :], contract, preferred_element_type=F32
            )
            hidden_product = lax.dot_general(
                hidden[e, left, :], hidden[e, right, :], contract, preferred_element_type=F32
            )
            both = rows_product * hidden_product
            if a != b:
                both = both + both
            folded = jnp.sum(both.reshape(part // 8, 8, part), axis=0)
            squares[...] += jnp.broadcast_to(jnp.sum(folded, axis=1, keepdims=True), (8, 128))
        return carry

    lax.fori_loop(0, experts, add_squares, 0)

    own_norm[0] = squares[...]

    def norm_copy(step, to_slot):
        return remote(
            own_norm.at[0], norm_dp.at[to_slot], norm_send.at[step], norm_recv.at[step],
            {"dp": (dp + step) % n_dp},
        )

    for step in range(1, n_dp):
        norm_copy(step, dp).start()
    norm_dp[dp] = own_norm[0]
    for e in range(experts):

        def turn(j, carry):
            at = pl.ds(pl.multiple_of(j * 128, 128), 128)
            hidden_t[e, at, :] = hidden[e, :, at].T
            return carry

        lax.fori_loop(0, units // 128, turn, 0)
    for step in range(1, n_dp):
        norm_copy(step, (dp - step + n_dp) % n_dp).wait_recv()
    total = norm_dp[0]
    for i in range(1, n_dp):
        total = total + norm_dp[i]
    own_norm[1] = total
    core_norm = remote(
        own_norm.at[1], norm_core, norm_send.at[0], norm_recv.at[0], {"expert": 1 - core}
    )
    core_norm.start()
    core_norm.wait()
    own_norm[2] = total + norm_core[...]
    pair_norm = remote(
        own_norm.at[2], norm_pair, norm_send.at[n_dp], norm_recv.at[n_dp], {"ffn": 1 - side}
    )
    pair_norm.start()

    pair_norm.wait()
    norm_ref[...] = own_norm[2] + norm_pair[...]

    for index in range(groups_own):
        for e in range(experts):
            part_copy(index, e).wait()
    for step in range(1, n_dp):
        meta_copy(step, dp).wait_send()
        norm_copy(step, dp).wait_send()

    def drain(g, carry):
        @pl.when((z < n_z - 1) & (g <= z))
        def _():
            z_copy(g, True).wait_send()

        @pl.when((z > 0) & (g >= z))
        def _():
            z_copy(g, False).wait_send()

        x_copy(g, x).wait_send()

        @pl.when(g != z)
        def _():
            core_copy(g, x, core).wait_send()

        core_copy(g, 1 - x, core).wait_send()
        return carry

    lax.fori_loop(0, n_z, drain, 0)


def fused_call(n_dp, ids, probs, grad_rows, gate_pre, up_pre, down_weight):
    experts, own_slots, units = gate_pre.shape
    block, width = grad_rows.shape
    n_z = n_dp // 2
    groups_own = n_z // 2
    slots = n_dp * CAP
    vmem = pl.BlockSpec(memory_space=pltpu.VMEM)
    hbm = pl.BlockSpec(memory_space=pl.ANY)
    dma = pltpu.SemaphoreType.DMA
    return pl.pallas_call(
        functools.partial(fused_kernel, n_dp),
        out_shape=(
            pltpu.VMEM((experts, slots, width), BF16),
            pltpu.VMEM((experts, units, slots), BF16),
            pltpu.VMEM(gate_pre.shape, BF16),
            pltpu.VMEM(gate_pre.shape, BF16),
            pltpu.VMEM((8, 128), F32),
        ),
        in_specs=[vmem, vmem, hbm, vmem, vmem, hbm],
        out_specs=(vmem,) * 5,
        scratch_shapes=[
            pltpu.VMEM((n_z, 2 * block, width), BF16),
            pltpu.VMEM((n_dp, 8, block), F32),
            pltpu.VMEM(down_weight.shape, BF16),
            pltpu.VMEM((experts, slots, units), BF16),
            pltpu.VMEM(gate_pre.shape, BF16),
            pltpu.VMEM((8, 128), F32),
            pltpu.VMEM((n_dp, 8, 128), F32),
            pltpu.VMEM((8, 128), F32),
            pltpu.VMEM((8, 128), F32),
            pltpu.VMEM((3, 8, 128), F32),
            dma((2,)),
            dma((n_dp,)),
            dma((n_dp,)),
            dma((2, n_z)),
            dma((n_z,)),
            dma((n_z,)),
            dma((n_z,)),
            dma((n_z, 2)),
            dma((n_z, 2)),
            dma((experts,)),
            dma((experts,)),
            dma((groups_own, experts)),
            dma((groups_own, experts)),
            dma((n_dp + 1,)),
            dma((n_dp + 1,)),
        ],
        compiler_params=pltpu.CompilerParams(
            collective_id=0, has_side_effects=True, vmem_limit_bytes=47 * 1024 * 1024
        ),
    )(ids, probs, grad_rows, gate_pre, up_pre, down_weight)


def finish_kernel(
    clip_limit, norm_ref, hidden_ref, placed_ref, gate_ref, up_ref, mine_ref, theirs_ref,
    wide_out, gate_out, up_out,
):
    squares = jnp.sum(jnp.sum(norm_ref[...], axis=0, keepdims=True), axis=1, keepdims=True) / 128.0
    factor = clip_limit / jnp.maximum(jnp.sqrt(squares), clip_limit)
    e, j = pl.program_id(0), pl.program_id(1)
    units, tile = wide_out.shape[1], wide_out.shape[2]
    piece = gate_out.shape[1]
    half_units = units // 2
    for a in range(2):
        at = pl.ds(a * half_units, half_units)
        product = jnp.dot(
            hidden_ref[e, at, :], placed_ref[e, :, pl.ds(pl.multiple_of(j * tile, 128), tile)],
            preferred_element_type=F32,
        )
        wide_out[0, at, :] = (product * factor).astype(BF16)
    rows = pl.ds(pl.multiple_of(j * piece, 16), piece)
    gate = gate_ref[0].astype(F32)
    up = up_ref[0].astype(F32)
    grad = mine_ref[e, rows, :].astype(F32) + theirs_ref[e, rows, :].astype(F32)
    sig = jax.nn.sigmoid(gate)
    gate_out[0] = (grad * up * sig * (1.0 + gate * (1.0 - sig))).astype(BF16)
    up_out[0] = (grad * (gate * sig)).astype(BF16)


def finish_call(clip_limit, norm, hidden_t, placed, gate_pre, up_pre, mine, theirs):
    experts, units, slots = hidden_t.shape
    width = placed.shape[2]
    steps = 6
    tile, piece = width // steps, gate_pre.shape[1] // steps
    vmem = pl.BlockSpec(memory_space=pltpu.VMEM)
    rows = pl.BlockSpec((1, piece, units), lambda e, j: (e, j, 0))
    return pl.pallas_call(
        functools.partial(finish_kernel, clip_limit),
        grid=(experts, steps),
        out_shape=(
            jax.ShapeDtypeStruct((experts, units, width), BF16),
            jax.ShapeDtypeStruct(gate_pre.shape, BF16),
            jax.ShapeDtypeStruct(gate_pre.shape, BF16),
        ),
        in_specs=[
            vmem, vmem, vmem, rows, rows, vmem, vmem,
        ],
        out_specs=(pl.BlockSpec((1, units, tile), lambda e, j: (e, 0, j)), rows, rows),
        compiler_params=pltpu.CompilerParams(vmem_limit_bytes=24 * 1024 * 1024),
    )(norm, hidden_t, placed, gate_pre, up_pre, mine, theirs)


def fused_device(grad_rows, gate_probs, expert_ids, gate_pre, up_pre, down_weight):
    n_dp = lax.axis_size("dp")
    entry_count = (
        float(gate_pre.shape[0] * lax.axis_size("expert"))
        * float(gate_pre.shape[2] * n_dp)
        * float(down_weight.shape[2] * lax.axis_size("ffn"))
    )
    clip_limit = 0.5 * math.sqrt(entry_count)
    placed, hidden_t, mine, theirs, norm = fused_call(
        n_dp, expert_ids.T, gate_probs.T, grad_rows, gate_pre, up_pre, down_weight
    )
    return finish_call(clip_limit, norm, hidden_t, placed, gate_pre, up_pre, mine, theirs)


def solution(mesh):
    placed = (
        P("dp", "ffn"),
        P("dp", None),
        P("dp", None),
        P("expert", "ffn", "dp"),
        P("expert", "ffn", "dp"),
        P("expert", "dp", "ffn"),
    )
    fits = mesh.shape["dp"] == 8 and mesh.shape["expert"] == 2 and mesh.shape["ffn"] == 2
    return jax.shard_map(
        fused_device if fits else on_device,
        mesh=mesh,
        in_specs=placed,
        out_specs=(P("expert", "dp", "ffn"), P("expert", "ffn", "dp"), P("expert", "ffn", "dp")),
        check_vma=False,
    )
```

```python
import functools
import math

import jax
import jax.numpy as jnp
from jax import lax
from jax.experimental import pallas as pl
from jax.experimental.pallas import tpu as pltpu
from jax.sharding import PartitionSpec as P

CAP = 72
MESH = pl.DeviceIdType.MESH
F32 = jnp.float32
BF16 = jnp.bfloat16


def slot_table(route_ids, experts_total):
    tokens_here, routes = route_ids.shape
    flat_ids = route_ids.reshape(tokens_here * routes)
    one_hot = (flat_ids[:, None] == jnp.arange(experts_total, dtype=jnp.int32)[None, :]).astype(
        jnp.int32
    )
    earlier = jnp.cumsum(one_hot, axis=0) - one_hot
    return jnp.sum(earlier * one_hot, axis=1).reshape(tokens_here, routes)


def on_device(grad_rows, gate_probs, expert_ids, gate_pre, up_pre, down_weight):
    experts_here, rows_here, hidden_width = gate_pre.shape
    feature_width = down_weight.shape[2]
    capacity = CAP
    experts_total = experts_here * lax.axis_size("expert")
    slot_index = slot_table(expert_ids, experts_total)
    first_expert = lax.axis_index("expert") * experts_here
    local_ids = expert_ids - first_expert
    expert_match = (
        local_ids[:, :, None] == jnp.arange(experts_here, dtype=jnp.int32)[None, None, :]
    ).astype(jnp.float32)
    expert_match = expert_match * gate_probs[:, :, None]
    slot_match = (
        slot_index[:, :, None] == jnp.arange(capacity, dtype=jnp.int32)[None, None, :]
    ).astype(jnp.float32)
    placing = jnp.einsum("tke,tks->est", expert_match, slot_match, precision=lax.Precision.HIGHEST)
    dispatched = jnp.einsum(
        "est,td->esd", placing, grad_rows.astype(jnp.float32), precision=lax.Precision.HIGHEST
    ).astype(jnp.bfloat16)
    arrived = lax.all_gather(dispatched, "dp", axis=1, tiled=True)
    gate_value = gate_pre.astype(jnp.float32)
    up_value = up_pre.astype(jnp.float32)
    sigmoid_gate = jax.nn.sigmoid(gate_value)
    silu_gate = gate_value * sigmoid_gate
    hidden = (silu_gate * up_value).astype(jnp.bfloat16)
    partial_sums = jnp.einsum(
        "erd,efd->erf", arrived, down_weight, preferred_element_type=jnp.float32
    )
    own_rows = lax.psum_scatter(
        partial_sums.astype(jnp.bfloat16), "ffn", scatter_dimension=1, tiled=True
    ).astype(jnp.float32)
    gate_grad = (
        own_rows * up_value * sigmoid_gate * (1.0 + gate_value * (1.0 - sigmoid_gate))
    ).astype(jnp.bfloat16)
    up_grad = (own_rows * silu_gate).astype(jnp.bfloat16)
    weight_grad = jnp.einsum(
        "erf,erd->efd",
        lax.all_gather(hidden, "ffn", axis=1, tiled=True),
        arrived,
        preferred_element_type=jnp.float32,
    )
    squares = lax.psum(jnp.sum(weight_grad * weight_grad), ("dp", "expert", "ffn"))
    entry_count = (
        float(experts_total)
        * float(hidden_width * lax.axis_size("dp"))
        * float(feature_width * lax.axis_size("ffn"))
    )
    clip_limit = jnp.float32(0.5 * math.sqrt(entry_count))
    factor = clip_limit / jnp.maximum(jnp.sqrt(squares), clip_limit)
    down_grad = (weight_grad * factor).astype(jnp.bfloat16)
    return (down_grad, gate_grad, up_grad)


def fused_kernel(
    n_dp, ids_ref, probs_ref, rows_ref, gate_ref, up_ref, weight_ref,
    placed, hidden_t, mine, incoming, wide_low, wide_high, norm_ref,
    tokens, metas, weight, hidden, outgoing,
    squares, norm_dp, norm_core, norm_pair, own_norm,
    load_sem, meta_send, meta_recv, z_send, z_recv, x_send, x_recv, core_send, core_recv,
    hidden_send, hidden_recv, part_send, part_recv, norm_send, norm_recv,
):
    dp = lax.axis_index("dp")
    core = lax.axis_index("expert")
    side = lax.axis_index("ffn")
    n_z = n_dp // 2
    z, x = dp // 2, dp % 2
    experts, own_slots, units = gate_ref.shape
    block = rows_ref.shape[0]
    half = block // 2
    width = rows_ref.shape[1]
    group = 2 * CAP
    groups_own = n_z // 2

    load_rows = pltpu.make_async_copy(
        rows_ref, tokens.at[z, pl.ds(pl.multiple_of(x * block, block), block), :], load_sem.at[0]
    )
    load_rows.start()
    load_weight = pltpu.make_async_copy(weight_ref, weight, load_sem.at[1])
    load_weight.start()

    barrier = pltpu.get_barrier_semaphore()
    for step in range(1, n_dp):
        pl.semaphore_signal(
            barrier, inc=1, device_id={"dp": (dp + step) % n_dp}, device_id_type=MESH
        )
    pl.semaphore_signal(barrier, inc=1, device_id={"expert": 1 - core}, device_id_type=MESH)
    pl.semaphore_signal(barrier, inc=1, device_id={"ffn": 1 - side}, device_id_type=MESH)
    piece = 48

    def make_hidden(e):
        def hidden_piece(i, carry):
            start = pl.multiple_of(i * piece, 16)
            gate = gate_ref[e, pl.ds(start, piece), :].astype(F32)
            up = up_ref[e, pl.ds(start, piece), :].astype(F32)
            to = pl.multiple_of(side * own_slots + start, 16)
            hidden[e, pl.ds(to, piece), :] = (gate * jax.nn.sigmoid(gate) * up).astype(BF16)
            return carry

        lax.fori_loop(0, own_slots // piece, hidden_piece, 0)

    make_hidden(0)
    pl.semaphore_wait(barrier, n_dp + 1)

    def half_rows(z_of, x_of, core_of):
        start = pl.multiple_of(x_of * block + core_of * half, half)
        return tokens.at[z_of, pl.ds(start, half), :]

    def remote(src, dst, send, recv, to):
        return pltpu.make_async_remote_copy(
            src_ref=src, dst_ref=dst, send_sem=send, recv_sem=recv,
            device_id=to, device_id_type=MESH,
        )

    def z_copy(g, up):
        place = half_rows(g, x, core)
        to = jnp.clip(z + (1 if up else -1), 0, n_z - 1) * 2 + x
        return remote(place, place, z_send.at[1 if up else 0, g], z_recv.at[g], {"dp": to})

    def x_copy(g, x_of):
        place = half_rows(g, x_of, core)
        return remote(place, place, x_send.at[g], x_recv.at[g], {"dp": z * 2 + 1 - x})

    def core_copy(g, x_of, core_of):
        place = half_rows(g, x_of, core_of)
        return remote(
            place, place, core_send.at[g, x_of], core_recv.at[g, x_of], {"expert": 1 - core}
        )

    def meta_copy(step, source):
        return remote(
            metas.at[source], metas.at[source], meta_send.at[step], meta_recv.at[step],
            {"dp": (dp + step) % n_dp},
        )

    metas[dp] = jnp.concatenate(
        [ids_ref[...].astype(F32), probs_ref[...], jnp.zeros((4, block), F32)], axis=0
    )
    for step in range(1, n_dp):
        meta_copy(step, dp).start()
    load_rows.wait()

    @pl.when(z < n_z - 1)
    def _():
        z_copy(z, True).start()

    @pl.when(z > 0)
    def _():
        z_copy(z, False).start()

    x_copy(z, x).start()

    def hidden_copy(e, side_of):
        start = pl.multiple_of(side_of * own_slots, 16)
        place = hidden.at[e, pl.ds(start, own_slots), :]
        return remote(place, place, hidden_send.at[e], hidden_recv.at[e], {"ffn": 1 - side})

    hidden_copy(0, side).start()
    for e in range(1, experts):
        make_hidden(e)
        hidden_copy(e, side).start()

    for step in range(1, n_dp):
        meta_copy(step, (dp - step + n_dp) % n_dp).wait_recv()
    load_weight.wait()

    first = (core * experts).astype(F32)
    n_cols = 4
    cols = width // n_cols
    unit_cols = 256

    def part_copy(index, e):
        at = pl.ds(pl.multiple_of(index * group, 16), group)
        return remote(
            outgoing.at[e, at, :], incoming.at[e, at, :], part_send.at[index, e],
            part_recv.at[index, e], {"ffn": 1 - side},
        )

    def process(g):
        meta = jnp.concatenate([metas[2 * g], metas[2 * g + 1]], axis=1)
        lane = lax.broadcasted_iota(jnp.int32, (2 * block, 2 * block), 1)
        sub = lax.broadcasted_iota(jnp.int32, (2 * block, 2 * block), 0)
        before = jnp.where(
            (sub < lane) & ((sub >= block) == (lane >= block)), 1.0, 0.0
        ).astype(BF16)
        row = lax.broadcasted_iota(jnp.int32, (group, 2 * block), 0).astype(F32)
        offset = jnp.where(
            lax.broadcasted_iota(jnp.int32, (1, 2 * block), 1) >= block, float(CAP), 0.0
        )
        start = pl.multiple_of(g * group, 16)
        for e in range(experts):
            first_match = meta[0:1] == first + e
            second_match = meta[1:2] == first + e
            match = jnp.where(first_match | second_match, 1.0, 0.0)
            prob = jnp.where(first_match, meta[2:3], jnp.where(second_match, meta[3:4], 0.0))
            earlier = jnp.dot(
                jnp.broadcast_to(match, (16, 2 * block)).astype(BF16), before,
                preferred_element_type=F32,
            )[0:1]
            key = jnp.where(match > 0.0, earlier + offset, -1.0)
            chosen = row == key
            scale = jnp.sum(jnp.where(chosen, prob, 0.0), axis=1, keepdims=True)
            select = jnp.where(chosen, 1.0, 0.0).astype(BF16)

            def place_cols(j, carry):
                at = pl.ds(pl.multiple_of(j * cols, 128), cols)
                picked = jnp.dot(select, tokens[g, :, at], preferred_element_type=F32)
                placed[e, pl.ds(start, group), at] = (picked * scale).astype(BF16)
                return carry

            lax.fori_loop(0, n_cols, place_cols, 0)
        is_own = (g // groups_own) == side
        index = g % groups_own
        index_rows = pl.ds(pl.multiple_of(index * group, 16), group)
        for e in range(experts):

            def unit_tile(j, carry):
                at = pl.ds(pl.multiple_of(j * unit_cols, 128), unit_cols)
                term = lax.dot_general(
                    placed[e, pl.ds(start, group), :], weight[e, at, :],
                    (((1,), (1,)), ((), ())), preferred_element_type=F32,
                ).astype(BF16)

                @pl.when(is_own)
                def _():
                    mine[e, index_rows, at] = term

                @pl.when(jnp.logical_not(is_own))
                def _():
                    outgoing[e, index_rows, at] = term

                return carry

            lax.fori_loop(0, units // unit_cols, unit_tile, 0)

            @pl.when(jnp.logical_not(is_own))
            def _():
                part_copy(index, e).start()

    def stage(s, carry):
        for sign in (-1, 1):
            g = z + sign * (s + 1)
            onward = z - sign

            @pl.when((g >= 0) & (g < n_z))
            def _():
                z_copy(g, sign < 0).wait_recv()

                @pl.when((onward >= 0) & (onward < n_z))
                def _():
                    z_copy(g, sign < 0).start()

                x_copy(g, x).start()
                core_copy(g, x, core).start()

        for sign in (-1, 1):
            g = z + sign * s

            @pl.when((g >= 0) & (g < n_z) & ((s > 0) | (sign < 0)))
            def _():
                x_copy(g, 1 - x).wait_recv()
                core_copy(g, 1 - x, core).start()

        def side_of_stage(k, inner):
            g = z + (2 * k - 1) * s

            @pl.when((g >= 0) & (g < n_z) & ((s > 0) | (k == 0)))
            def _():
                @pl.when(s > 0)
                def _():
                    core_copy(g, x, 1 - core).wait_recv()

                core_copy(g, 1 - x, 1 - core).wait_recv()
                process(g)

            return inner

        lax.fori_loop(0, 2, side_of_stage, 0)
        return carry

    lax.fori_loop(0, n_z, stage, 0)

    for e in range(experts):
        hidden_copy(e, 1 - side).wait_recv()
        hidden_copy(e, side).wait_send()

    squares[...] = jnp.zeros_like(squares)
    slots = hidden.shape[1]
    part = slots // 2
    contract = (((1,), (1,)), ((), ()))

    def add_squares(e, carry):
        for a, b in ((0, 0), (0, 1), (1, 1)):
            left, right = pl.ds(a * part, part), pl.ds(b * part, part)
            rows_product = lax.dot_general(
                placed[e, left, :], placed[e, right, :], contract, preferred_element_type=F32
            )
            hidden_product = lax.dot_general(
                hidden[e, left, :], hidden[e, right, :], contract, preferred_element_type=F32
            )
            both = rows_product * hidden_product
            if a != b:
                both = both + both
            folded = jnp.sum(both.reshape(part // 8, 8, part), axis=0)
            squares[...] += jnp.broadcast_to(jnp.sum(folded, axis=1, keepdims=True), (8, 128))
        return carry

    lax.fori_loop(0, experts, add_squares, 0)

    own_norm[0] = squares[...]

    def norm_copy(step, to_slot):
        return remote(
            own_norm.at[0], norm_dp.at[to_slot], norm_send.at[step], norm_recv.at[step],
            {"dp": (dp + step) % n_dp},
        )

    for step in range(1, n_dp):
        norm_copy(step, dp).start()
    norm_dp[dp] = own_norm[0]

    wide_cols = 256
    wide_tiles = width // wide_cols

    def wide_half(wide_ref, first_tile):
        def wide_tile(j, carry):
            at = pl.ds(pl.multiple_of(j * wide_cols, 128), wide_cols)
            source = pl.ds(pl.multiple_of((first_tile + j) * wide_cols, 128), wide_cols)
            product = jnp.dot(hidden_t[0], placed[0, :, source], preferred_element_type=F32)
            wide_ref[:, at] = product.astype(BF16)
            return carry

        lax.fori_loop(0, wide_tiles // 2, wide_tile, 0)

    for e in range(experts):

        def turn(j, carry):
            at = pl.ds(pl.multiple_of(j * 128, 128), 128)
            hidden_t[e, at, :] = hidden[e, :, at].T
            return carry

        lax.fori_loop(0, units // 128, turn, 0)
    for step in range(1, n_dp):
        norm_copy(step, (dp - step + n_dp) % n_dp).wait_recv()
    total = norm_dp[0]
    for i in range(1, n_dp):
        total = total + norm_dp[i]
    own_norm[1] = total
    core_norm = remote(
        own_norm.at[1], norm_core, norm_send.at[0], norm_recv.at[0], {"expert": 1 - core}
    )
    core_norm.start()
    wide_half(wide_low, 0)
    core_norm.wait()
    own_norm[2] = total + norm_core[...]
    pair_norm = remote(
        own_norm.at[2], norm_pair, norm_send.at[n_dp], norm_recv.at[n_dp], {"ffn": 1 - side}
    )
    pair_norm.start()
    wide_half(wide_high, wide_tiles // 2)

    pair_norm.wait()
    norm_ref[...] = own_norm[2] + norm_pair[...]

    for index in range(groups_own):
        for e in range(experts):
            part_copy(index, e).wait()
    for step in range(1, n_dp):
        meta_copy(step, dp).wait_send()
        norm_copy(step, dp).wait_send()

    def drain(g, carry):
        @pl.when((z < n_z - 1) & (g <= z))
        def _():
            z_copy(g, True).wait_send()

        @pl.when((z > 0) & (g >= z))
        def _():
            z_copy(g, False).wait_send()

        x_copy(g, x).wait_send()

        @pl.when(g != z)
        def _():
            core_copy(g, x, core).wait_send()

        core_copy(g, 1 - x, core).wait_send()
        return carry

    lax.fori_loop(0, n_z, drain, 0)


def fused_call(n_dp, ids, probs, grad_rows, gate_pre, up_pre, down_weight):
    experts, own_slots, units = gate_pre.shape
    block, width = grad_rows.shape
    n_z = n_dp // 2
    groups_own = n_z // 2
    slots = n_dp * CAP
    vmem = pl.BlockSpec(memory_space=pltpu.VMEM)
    hbm = pl.BlockSpec(memory_space=pl.ANY)
    dma = pltpu.SemaphoreType.DMA
    return pl.pallas_call(
        functools.partial(fused_kernel, n_dp),
        out_shape=(
            pltpu.VMEM((experts, slots, width), BF16),
            pltpu.VMEM((experts, units, slots), BF16),
            pltpu.VMEM(gate_pre.shape, BF16),
            pltpu.VMEM(gate_pre.shape, BF16),
            pltpu.VMEM((units, width // 2), BF16),
            pltpu.VMEM((units, width // 2), BF16),
            pltpu.VMEM((8, 128), F32),
        ),
        in_specs=[vmem, vmem, hbm, vmem, vmem, hbm],
        out_specs=(vmem,) * 7,
        scratch_shapes=[
            pltpu.VMEM((n_z, 2 * block, width), BF16),
            pltpu.VMEM((n_dp, 8, block), F32),
            pltpu.VMEM(down_weight.shape, BF16),
            pltpu.VMEM((experts, slots, units), BF16),
            pltpu.VMEM(gate_pre.shape, BF16),
            pltpu.VMEM((8, 128), F32),
            pltpu.VMEM((n_dp, 8, 128), F32),
            pltpu.VMEM((8, 128), F32),
            pltpu.VMEM((8, 128), F32),
            pltpu.VMEM((3, 8, 128), F32),
            dma((2,)),
            dma((n_dp,)),
            dma((n_dp,)),
            dma((2, n_z)),
            dma((n_z,)),
            dma((n_z,)),
            dma((n_z,)),
            dma((n_z, 2)),
            dma((n_z, 2)),
            dma((experts,)),
            dma((experts,)),
            dma((groups_own, experts)),
            dma((groups_own, experts)),
            dma((n_dp + 1,)),
            dma((n_dp + 1,)),
        ],
        compiler_params=pltpu.CompilerParams(
            collective_id=0, has_side_effects=True, vmem_limit_bytes=33 * 1024 * 1024
        ),
    )(ids, probs, grad_rows, gate_pre, up_pre, down_weight)


def finish_kernel(
    clip_limit, norm_ref, low_ref, high_ref, hidden_ref, placed_ref, gate_ref, up_ref, mine_ref, theirs_ref,
    wide_out, gate_out, up_out,
):
    squares = jnp.sum(jnp.sum(norm_ref[...], axis=0, keepdims=True), axis=1, keepdims=True) / 128.0
    factor = clip_limit / jnp.maximum(jnp.sqrt(squares), clip_limit)
    j, e = pl.program_id(0), pl.program_id(1)
    units, tile = wide_out.shape[1], wide_out.shape[2]
    piece = gate_out.shape[1]
    half_units = units // 2
    cols = pl.ds(pl.multiple_of(j * tile, 128), tile)

    half_steps = pl.num_programs(0) // 2
    for k, wide_ref in enumerate((low_ref, high_ref)):

        @pl.when((e == 0) & (j // half_steps == k))
        def _():
            at = pl.ds(pl.multiple_of((j - k * half_steps) * tile, 128), tile)
            wide_out[0] = (wide_ref[:, at].astype(F32) * factor).astype(BF16)

    @pl.when(e > 0)
    def _():
        for a in range(2):
            at = pl.ds(a * half_units, half_units)
            product = jnp.dot(
                hidden_ref[e, at, :], placed_ref[e, :, cols], preferred_element_type=F32
            )
            wide_out[0, at, :] = (product * factor).astype(BF16)

    rows = pl.ds(pl.multiple_of(j * piece, 16), piece)
    gate = gate_ref[0].astype(F32)
    up = up_ref[0].astype(F32)
    grad = mine_ref[e, rows, :].astype(F32) + theirs_ref[e, rows, :].astype(F32)
    sig = jax.nn.sigmoid(gate)
    gate_out[0] = (grad * up * sig * (1.0 + gate * (1.0 - sig))).astype(BF16)
    up_out[0] = (grad * (gate * sig)).astype(BF16)


def finish_call(clip_limit, norm, low, high, hidden_t, placed, gate_pre, up_pre, mine, theirs):
    experts, units, slots = hidden_t.shape
    width = placed.shape[2]
    steps = 6
    tile, piece = width // steps, gate_pre.shape[1] // steps
    vmem = pl.BlockSpec(memory_space=pltpu.VMEM)
    rows = pl.BlockSpec((1, piece, units), lambda j, e: (e, j, 0))
    return pl.pallas_call(
        functools.partial(finish_kernel, clip_limit),
        grid=(steps, experts),
        out_shape=(
            jax.ShapeDtypeStruct((experts, units, width), BF16),
            jax.ShapeDtypeStruct(gate_pre.shape, BF16),
            jax.ShapeDtypeStruct(gate_pre.shape, BF16),
        ),
        in_specs=[
            vmem, vmem, vmem, vmem, vmem, rows, rows, vmem, vmem,
        ],
        out_specs=(pl.BlockSpec((1, units, tile), lambda j, e: (e, 0, j)), rows, rows),
        compiler_params=pltpu.CompilerParams(vmem_limit_bytes=24 * 1024 * 1024),
    )(norm, low, high, hidden_t, placed, gate_pre, up_pre, mine, theirs)


def fused_device(grad_rows, gate_probs, expert_ids, gate_pre, up_pre, down_weight):
    n_dp = lax.axis_size("dp")
    entry_count = (
        float(gate_pre.shape[0] * lax.axis_size("expert"))
        * float(gate_pre.shape[2] * n_dp)
        * float(down_weight.shape[2] * lax.axis_size("ffn"))
    )
    clip_limit = 0.5 * math.sqrt(entry_count)
    placed, hidden_t, mine, theirs, low, high, norm = fused_call(
        n_dp, expert_ids.T, gate_probs.T, grad_rows, gate_pre, up_pre, down_weight
    )
    return finish_call(
        clip_limit, norm, low, high, hidden_t, placed, gate_pre, up_pre, mine, theirs
    )


def solution(mesh):
    placed = (
        P("dp", "ffn"),
        P("dp", None),
        P("dp", None),
        P("expert", "ffn", "dp"),
        P("expert", "ffn", "dp"),
        P("expert", "dp", "ffn"),
    )
    fits = mesh.shape["dp"] == 8 and mesh.shape["expert"] == 2 and mesh.shape["ffn"] == 2
    return jax.shard_map(
        fused_device if fits else on_device,
        mesh=mesh,
        in_specs=placed,
        out_specs=(P("expert", "dp", "ffn"), P("expert", "ffn", "dp"), P("expert", "ffn", "dp")),
        check_vma=False,
    )
```
